256 devices in a mesh: row: 16 (over y, z_lo, core), col: 4 (over z_hi), hour: 4 (over x).
Axes of the slice: x: 4, y: 4, z: 8 (z_hi: 4, z_lo: 2; z = z_hi * 2 + z_lo), core: 2. Of those that a mesh axis runs over, the one named last changes fastest.
Arguments:
- spectra: bfloat16 [8, 2, 256, 8192], P(None, None, 'hour', ('row', 'col')), may hold values from -6 to 6
- quality: int32 [256], P('hour'), may hold values 0 or 1
- column_blocks: int32 [16], replicated, may hold values from 0 to 15, each once
Outputs:
- cross: bfloat16 [8, 2, 8192, 8192], P('hour', None, 'row', 'col')
The draws below stay inside these ranges and needn't reach their ends.
Inputs may be any that keep to these rules, and one draw needn't show every extreme that they name: `column_blocks`: each channel block appears once.
All inputs are finite; a program needn't handle non-finite values. No bound on the sum of `quality` on one device may be relied on, other than what follows from the above.
Results may differ from the reference program's by a relative error of at most 0.012.
Values may be sent and summed in bfloat16 or wider, within the bound.
No kernel may reach another device: no remote copies, remote signals or barrier semaphores. Data moves between devices by JAX's collectives and lax.ppermute only.
A program may use at most 256 MiB of HBM per device.

```python
import jax
import jax.numpy as jnp
from jax import lax

F = 8
CB = 512
W_DEV = 64
NB = 16
CH = 8192
W = 256
N_HOUR = 4


def with_ends(values, rng, smallest, top_value):
    index_at = [jax.random.randint(jax.random.fold_in(rng, axis), (), 0, length) for axis, length in enumerate(values.shape)]
    widest = values.shape.index(max(values.shape))
    beside = index_at[:widest] + [(index_at[widest] + 1) % values.shape[widest]] + index_at[widest + 1:]
    return values.at[tuple(index_at)].set(smallest).at[tuple(beside)].set(top_value)


def steps_of(stream_key, shape, shards, low, high):
    factor_of = 1.0
    for axis_at, parts in shards:
        steps = jax.random.uniform(jax.random.fold_in(jax.random.fold_in(stream_key, 6), axis_at), (parts,), jnp.float32, low / len(shards), high / len(shards))
        factor_of = factor_of * jnp.repeat(jnp.exp(steps), shape[axis_at] // parts).reshape((-1,) + (1,) * (len(shape) - 1 - axis_at))
    return factor_of


def normal_values(stream_key, extent, width, reach, split=(), dtype=jnp.bfloat16):
    array = jax.random.normal(stream_key, extent, jnp.float32) * width
    if len(split) > 0:
        array = steps_of(stream_key, extent, split, -0.22, 0.18) * array
    return jnp.clip(array, min=-reach, max=reach).astype(dtype)


def setup_inputs(seed: int = 0) -> dict:
    key_list = jax.random.split(jax.random.key(seed), 4)
    spectra = normal_values(key_list[0], (F, 2, W, CH), 1.0, 6.0, ((2, 4), (3, 64)))
    quality = with_ends((jax.random.randint(key_list[1], (W,), 0, 5) < 3).astype(jnp.int32), jax.random.fold_in(key_list[1], 1), 0, 1)
    column_blocks = jax.random.permutation(key_list[2], NB).astype(jnp.int32)
    return {"spectra": spectra, "quality": quality, "column_blocks": column_blocks}


def whiten(spectra, quality):
    values = spectra.astype(jnp.float32)
    power = lax.optimization_barrier(jnp.mean(values * values, axis=(0, 1)))
    keep = quality.astype(jnp.float32)[None, None, :, None]
    return (values * keep * lax.rsqrt(power + 1e-06)[None, None]).astype(jnp.bfloat16)

def pair_terms(left, right):
    real_part = jnp.dot(left[0].T, right[0], preferred_element_type=jnp.float32) + jnp.dot(left[1].T, right[1], preferred_element_type=jnp.float32)
    imag_part = jnp.dot(left[1].T, right[0], preferred_element_type=jnp.float32) - jnp.dot(left[0].T, right[1], preferred_element_type=jnp.float32)
    return jnp.stack([real_part, imag_part])

def one_bin(pair):
    left, right = pair
    factor = 1.0 / jnp.sqrt(jnp.float32(W))
    total = jnp.zeros((2, CH, CH), jnp.float32)
    for group in range(N_HOUR):
        part = pair_terms(left[:, group * W_DEV:(group + 1) * W_DEV], right[:, group * W_DEV:(group + 1) * W_DEV]) * factor
        rounded = lax.optimization_barrier(part.astype(jnp.bfloat16))
        total = total + rounded.astype(jnp.float32)
    return total.astype(jnp.bfloat16)

def reference(spectra, quality, column_blocks):
    white = whiten(spectra, quality)
    blocks = white.reshape(F, 2, W, NB, CB)
    columns = jnp.take(blocks, column_blocks.astype(jnp.int32), axis=3).reshape(F, 2, W, CH)
    return lax.map(one_bin, (white, columns))
```

```python
import functools

import jax
import jax.numpy as jnp
from jax import lax
from jax.experimental import pallas as pl
from jax.experimental.pallas import tpu as pltpu
from jax.sharding import PartitionSpec as P

CB = 512
BF = jnp.bfloat16
VMEM = pl.BlockSpec(memory_space=pltpu.VMEM)
SMEM = pl.BlockSpec(memory_space=pltpu.SMEM)
LIMIT = 40 * 1024 * 1024


def struct(*shape):
    return jax.ShapeDtypeStruct(shape, BF)


def params():
    return pltpu.CompilerParams(vmem_limit_bytes=LIMIT)


def whiten_kernel(spectra, quality, white, spread):
    values = spectra[...].astype(jnp.float32)
    power = jnp.sum(jnp.sum(values * values, axis=0), axis=0) * (1.0 / 16.0)
    scale = lax.rsqrt(power + 1e-06)
    keep = quality[...].astype(jnp.float32)
    result = (values * keep[None, None] * scale[None, None]).astype(BF)
    white[...] = result
    for h in range(4):
        for k in range(2):
            for z in range(2):
                for y in range(4):
                    spread[h, y, z, k] = result[2 * h + k, z, 16 * y : 16 * y + 16]


def whiten(spectra, quality):
    return pl.pallas_call(
        whiten_kernel,
        out_shape=[struct(8, 2, 64, 128), struct(4, 4, 2, 2, 16, 128)],
        in_specs=[VMEM, VMEM],
        out_specs=[VMEM, VMEM],
        compiler_params=params(),
        name="whiten",
    )(spectra, quality.reshape(64, 1))


def select_kernel(col, blocks, pieces, *refs):
    outs = refs[-4:]
    for d in range(4):
        group = lax.rem(col[0] + d, 4)
        for s in range(4):
            index = blocks[group * 4 + s]
            for h in range(4):
                outs[d][16 * h : 16 * h + 16, 128 * s : 128 * s + 128] = pieces[h, index]


def select(col, blocks, pieces, after):
    return pl.pallas_call(
        select_kernel,
        out_shape=[struct(64, 512)] * 4,
        in_specs=[SMEM, SMEM, VMEM] + [pl.BlockSpec(memory_space=pl.ANY)] * len(after),
        out_specs=[VMEM] * 4,
        compiler_params=params(),
        name="select",
    )(col, blocks, pieces, *after)


def merge_kernel(col, *refs):
    out = refs[4]
    for d in range(4):
        quarter = lax.rem(col[0] + d, 4)
        for s in range(4):
            at = pl.multiple_of(s * 512 + quarter * 128, 128)
            out[:, pl.ds(at, 128)] = refs[d][:, 128 * s : 128 * s + 128]


def merge(col, parts):
    return pl.pallas_call(
        merge_kernel,
        out_shape=struct(64, 2048),
        in_specs=[SMEM] + [VMEM] * 4,
        out_specs=VMEM,
        compiler_params=params(),
        name="merge",
    )(col, *parts)


def stack_kernel(count, *refs):
    out = refs[-1]
    at = 0
    for ref in refs[:count]:
        rows = ref.shape[0]
        out[at : at + rows] = ref[...]
        at += rows


def stack(parts, after=()):
    return pl.pallas_call(
        functools.partial(stack_kernel, len(parts)),
        out_shape=struct(sum(p.shape[0] for p in parts), parts[0].shape[1]),
        in_specs=[VMEM] * len(parts) + [pl.BlockSpec(memory_space=pl.ANY)] * len(after),
        out_specs=VMEM,
        compiler_params=params(),
        name="stack",
    )(*parts, *after)


def rows_out_kernel(place, own, before, after, far_low, far_high, *outs):
    col, hour = place[0], place[1]
    for d in range(4):
        pair = lax.rem(hour + d, 4)
        for ref, shift in ((own, 0), (after, 1), (before, 3)):
            quarter = lax.rem(col + shift, 4)
            outs[d][quarter] = ref[pl.ds(pair * 2, 2)]
        quarter = lax.rem(col + 2, 4)

        @pl.when(pair < 2)
        def _():
            outs[d][quarter] = far_low[pl.ds(lax.rem(pair, 2) * 2, 2)]

        @pl.when(pair >= 2)
        def _():
            outs[d][quarter] = far_high[pl.ds(lax.rem(pair, 2) * 2, 2)]


def rows_out(place, *refs):
    return pl.pallas_call(
        rows_out_kernel,
        out_shape=[struct(4, 2, 2, 64, 128)] * 4,
        in_specs=[SMEM] + [VMEM] * 5,
        out_specs=[VMEM] * 4,
        compiler_params=params(),
        name="rows_out",
    )(place, *refs)


def rows_in_kernel(place, *refs):
    out, held = refs[4], refs[5]
    for f in range(2):
        for p in range(2):
            for d in range(4):
                hour = lax.rem(place[1] + 4 - d, 4)
                for y in range(4):
                    at = pl.multiple_of(y * 64 + hour * 16, 16)
                    for q in range(4):
                        held[f, p, pl.ds(at, 16), 128 * q : 128 * q + 128] = refs[d][q, f, p, 16 * y : 16 * y + 16]
    for f in range(2):
        for p in range(2):
            out[f, p] = held[f, p].T


def rows_in(place, parts):
    return pl.pallas_call(
        rows_in_kernel,
        out_shape=struct(2, 2, 512, 256),
        in_specs=[SMEM] + [VMEM] * 4,
        out_specs=VMEM,
        scratch_shapes=[pltpu.VMEM((2, 2, 256, 512), BF)],
        compiler_params=params(),
        name="rows_in",
    )(place, *parts)


def product_kernel(place, left, near, far, *refs):
    out, held = refs[-2], refs[-1]
    y, z = place[0], place[1]
    spots = [(near, 0, 0), (near, 0, 1), (near, 3, 0), (near, 1, 0), (far, 3, 1), (far, 1, 1), (far, 2, 0), (far, 2, 1)]
    for i, (ref, dy, dz) in enumerate(spots):
        part = lax.rem(z + dz, 2)
        at = pl.multiple_of(lax.rem(y + dy, 4) * 64, 64)
        held[part, pl.ds(at, 64)] = ref[64 * (i % 4) : 64 * (i % 4) + 64]
    dot = functools.partial(jnp.dot, preferred_element_type=jnp.float32)
    factor = 1.0 / 16.0
    l0, l1 = left[0, 0], left[0, 1]
    r0, r1 = held[0], held[1]
    out[0, 0] = ((dot(l0, r0) + dot(l1, r1)) * factor).astype(BF)
    out[0, 1] = ((dot(l1, r0) - dot(l0, r1)) * factor).astype(BF)


def product(place, left, near, far, into=None):
    wide = 512
    extra = [] if into is None else [into]
    return pl.pallas_call(
        product_kernel,
        out_shape=struct(2, 2, 512, 2048),
        grid_spec=pltpu.PrefetchScalarGridSpec(
            num_scalar_prefetch=1,
            grid=(2048 // wide,),
            in_specs=[
                pl.BlockSpec((1, 2, 512, 256), lambda j, place: (place[2], 0, 0, 0)),
                pl.BlockSpec((256, wide), lambda j, place: (0, j)),
                pl.BlockSpec((256, wide), lambda j, place: (0, j)),
            ]
            + [pl.BlockSpec(memory_space=pl.ANY)] * len(extra),
            out_specs=pl.BlockSpec((1, 2, 512, wide), lambda j, place: (place[2], 0, 0, j)),
            scratch_shapes=[pltpu.VMEM((2, 256, wide), BF)],
        ),
        input_output_aliases={} if into is None else {4: 0},
        compiler_params=params(),
        cost_estimate=pl.CostEstimate(flops=2 * 4 * 512 * 256 * 2048, bytes_accessed=8 << 20, transcendentals=0),
        name="product",
    )(place, left, near, far, *extra)


def shift(value, axis, size, by):
    return lax.ppermute(value, axis, [(i, (i + by) % size) for i in range(size)])


def flip(value, bit):
    return lax.ppermute(value, "row", [(i, i ^ bit) for i in range(16)])


def per_device(spectra, quality, column_blocks):
    row, col, hour = (lax.axis_index(a) for a in ("row", "col", "hour"))
    y, z, k = row // 4, (row // 2) % 2, row % 2
    here = jnp.stack([col, hour]).astype(jnp.int32)
    white, spread = whiten(spectra, quality)

    before = shift(white, "col", 4, 1)
    after = shift(white, "col", 4, -1)

    pieces = lax.all_to_all(spread.reshape(64, 16, 128), ("hour", "row"), 0, 0, tiled=True)
    sent = select(here, column_blocks, pieces.reshape(4, 16, 16, 128), [before, after])
    from_before = shift(sent[1], "col", 4, 1)
    from_after = shift(sent[3], "col", 4, -1)
    from_far = shift(sent[2], "col", 4, 2)
    own = merge(here, [sent[0], from_after, from_far, from_before])

    far_low = shift(before[:4], "col", 4, 1)
    far_high = shift(after[4:], "col", 4, -1)
    own, far_low, far_high = lax.optimization_barrier((own, far_low, far_high))
    other = flip(own, 2)
    prev = shift(own, "row", 16, 4)
    succ = shift(own, "row", 16, -4)
    rows = rows_out(here, white, before, after, far_low, far_high)
    rows = [rows[0]] + [shift(rows[d], "hour", 4, d) for d in range(1, 4)]
    left = rows_in(here, rows)
    other_prev = shift(other, "row", 16, 4)
    other_succ = shift(other, "row", 16, -4)
    two_low = shift(prev[:32], "row", 16, 4)
    two_high = shift(succ[32:], "row", 16, -4)
    other_two_low = shift(other_prev[:32], "row", 16, 4)
    other_two_high = shift(other_succ[32:], "row", 16, -4)
    near = stack([own, other, prev, succ], rows[1:])
    far = stack([other_prev, other_succ, two_low, two_high, other_two_low, other_two_high])
    near_core = flip(near, 1)
    far_core = flip(far, 1)
    place = jnp.stack([y, z, k]).astype(jnp.int32)
    place_core = jnp.stack([y, z, 1 - k]).astype(jnp.int32)
    out = product(place, left, near, far)
    return product(place_core, left, near_core, far_core, out)


def solution(mesh):
    return jax.shard_map(
        per_device,
        mesh=mesh,
        in_specs=(P(None, None, "hour", ("row", "col")), P("hour"), P()),
        out_specs=P("hour", None, "row", "col"),
        check_vma=False,
    )
```

```python
import functools

import jax
import jax.numpy as jnp
from jax import lax
from jax.experimental import pallas as pl
from jax.experimental.pallas import tpu as pltpu
from jax.sharding import PartitionSpec as P

BF = jnp.bfloat16
VMEM = pl.BlockSpec(memory_space=pltpu.VMEM)
SMEM = pl.BlockSpec(memory_space=pltpu.SMEM)
ANY = pl.BlockSpec(memory_space=pl.ANY)


def struct(*shape):
    return jax.ShapeDtypeStruct(shape, BF)


def call(kernel, name, out_shape, in_specs, *operands, aliases={}, cost=None):
    return pl.pallas_call(
        kernel,
        out_shape=out_shape,
        input_output_aliases=aliases,
        in_specs=in_specs,
        out_specs=[VMEM] * len(out_shape) if isinstance(out_shape, list) else VMEM,
        compiler_params=pltpu.CompilerParams(vmem_limit_bytes=12 * 1024 * 1024),
        cost_estimate=cost,
        name=name,
    )(*operands)


def whiten_kernel(spectra, quality, white, spread):
    values = spectra[...].astype(jnp.float32)
    power = jnp.sum(jnp.sum(values * values, axis=0), axis=0) * (1.0 / 16.0)
    scale = lax.rsqrt(power + 1e-06)
    keep = jnp.broadcast_to(quality[...].astype(jnp.float32), (128, 64)).T
    result = (values * keep[None, None] * scale[None, None]).astype(BF)
    white[...] = result
    for h in range(4):
        for k in range(2):
            for z in range(2):
                for y in range(4):
                    spread[h, y, z, k] = result[2 * h + k, z, 16 * y : 16 * y + 16]


def whiten(spectra, quality):
    shapes = [struct(8, 2, 64, 128), struct(4, 4, 2, 2, 16, 128)]
    return call(whiten_kernel, "whiten", shapes, [VMEM] * 2, spectra, quality.reshape(1, 64))


def select_kernel(place, pieces, *outs):
    for d in range(4):
        group = place[0] ^ d
        for s in range(4):
            index = place[4 + group * 4 + s]
            for h in range(4):
                outs[d][16 * h : 16 * h + 16, 128 * s : 128 * s + 128] = pieces[h, index]


def select(place, pieces):
    return call(select_kernel, "select", [struct(64, 512)] * 4, [SMEM, VMEM], place, pieces)


def merge_kernel(place, *refs):
    out = refs[-1]
    for d in range(4):
        quarter = place[0] ^ d
        for s in range(4):
            at = pl.multiple_of(s * 512 + quarter * 128, 128)
            out[:, pl.ds(at, 128)] = refs[d][:, 128 * s : 128 * s + 128]


def merge(place, parts, after):
    specs = [SMEM] + [VMEM] * (4 + len(after))
    return call(merge_kernel, "merge", struct(64, 2048), specs, place, *parts, *after)


def relay_kernel(other, one, three, after, up, down):
    up[0:64] = other[...]
    up[64:96] = three[0:32]
    down[0:64] = other[...]
    down[64:96] = one[32:64]


def relay(*parts):
    return call(relay_kernel, "relay", [struct(96, 2048)] * 2, [VMEM] * 4, *parts)


def stack_kernel(*refs):
    out, at = refs[-1], 0
    for ref in refs[:-1]:
        rows = ref.shape[0]
        out[at : at + rows] = ref[...]
        at += rows


def stack(*parts):
    return call(stack_kernel, "stack", struct(256, 2048), [VMEM] * len(parts), *parts)


def hours_kernel(place, *refs):
    out = refs[-1]
    for d in range(4):
        hour = place[1] ^ d
        for i, dy in enumerate((0, 1, 3, 2)):
            at = pl.multiple_of(64 * i + hour * 16, 16)
            taken = pl.ds(pl.multiple_of((place[2] ^ dy) * 16, 16), 16)
            out[:, :, pl.ds(at, 16)] = refs[d][:, :, taken]


def hours(place, parts, after):
    specs = [SMEM] + [VMEM] * (4 + len(after))
    return call(hours_kernel, "hours", struct(2, 2, 256, 128), specs, place, *parts, *after)


WINDOWS = (
    (0, 0, 64), (1, 0, 64), (0, 64, 128), (0, 128, 192), (1, 64, 128),
    (0, 192, 224), (1, 128, 192), (0, 224, 256), (1, 192, 256),
)


def put_left(place, out, f, d, ref, ref_f):
    z = place[3]
    rows = ref[ref_f, z] * 0.0625, ref[ref_f, 1 - z] * 0.0625
    sign = jnp.where(z == 0, 1.0, -1.0)
    signed = (rows[1] * sign).astype(BF), (rows[0] * -sign).astype(BF)
    for part, of in enumerate((rows, signed)):
        ordered = jnp.concatenate([of[side][a:b] for side, a, b in WINDOWS], axis=0)
        out[f, part, 128 * d : 128 * d + 128] = ordered.T


def left_near_kernel(place, *refs):
    for d, ref in enumerate(refs[:3]):
        for f in range(2):
            put_left(place, refs[3], f, d, ref, f)


def left_near(place, *parts):
    return call(left_near_kernel, "left_near", struct(2, 2, 512, 512), [SMEM] + [VMEM] * 3, place, *parts)


def left_far_kernel(place, low, high, left, out):
    for f, ref in enumerate((low, high)):
        put_left(place, out, f, 3, ref, 0)


def left_far(place, *parts):
    cost = pl.CostEstimate(flops=50_000_000_000, bytes_accessed=1 << 20, transcendentals=0)
    specs, shape = [SMEM] + [VMEM] * 3, struct(2, 2, 512, 512)
    return call(left_far_kernel, "left_far", shape, specs, place, *parts, aliases={3: 0}, cost=cost)


WIDE, STRIPS = 512, 4


def product_kernel(place, left, *refs):
    out, held, sem = refs[4:]
    copies = []
    for n in range(2):
        near, far = refs[2 * n : 2 * n + 2]
        f = place[1] if n == 0 else 1 - place[1]
        both = left[f].reshape(1024, 512)
        for j in range(STRIPS):
            columns = slice(WIDE * j, WIDE * j + WIDE)
            right = jnp.concatenate([near[:, columns], far[:, columns]], axis=0)
            result = jnp.dot(both, right, preferred_element_type=jnp.float32)
            held[n, j] = result.astype(BF).reshape(2, 512, WIDE)
            for i, d in enumerate((0, 1, 3, 2)):
                rows = pl.ds(pl.multiple_of((place[0] ^ d) * 128, 128), 128)
                copy = pltpu.make_async_copy(
                    held.at[n, j, :, pl.ds(128 * i, 128)], out.at[f, :, rows, columns], sem.at[n, j, i]
                )
                copy.start()
                copies.append(copy)
    for copy in copies:
        copy.wait()


def product(*operands):
    return pl.pallas_call(
        product_kernel,
        out_shape=struct(2, 2, 512, 2048),
        in_specs=[SMEM] + [VMEM] * 5,
        out_specs=ANY,
        scratch_shapes=[
            pltpu.VMEM((2, STRIPS, 2, 512, WIDE), BF),
            pltpu.SemaphoreType.DMA((2, STRIPS, 4)),
        ],
        compiler_params=pltpu.CompilerParams(vmem_limit_bytes=16 * 1024 * 1024),
        name="product",
    )(*operands)


def swap(value, axis, bits):
    return lax.ppermute(value, axis, [(i, i ^ bits) for i in range(lax.axis_size(axis))])


def per_device(spectra, quality, column_blocks):
    row, col, hour = (lax.axis_index(a) for a in ("row", "col", "hour"))
    y, z, k = row // 4, (row // 2) % 2, row % 2
    place = jnp.concatenate([jnp.stack([col, hour, y, z]).astype(jnp.int32), column_blocks])
    white, spread = whiten(spectra, quality)
    parts = [lax.dynamic_slice_in_dim(white, 2 * (hour ^ d), 2, 0) for d in range(4)]
    parts = [parts[0]] + [swap(parts[d], "hour", d) for d in range(1, 4)]

    pieces = lax.all_to_all(spread.reshape(64, 16, 128), ("hour", "row"), 0, 0, tiled=True)
    sent = select(place, pieces.reshape(4, 16, 16, 128))
    sent = [sent[0]] + [swap(sent[d], "col", d) for d in range(1, 4)]
    own = merge(place, sent, parts[1:])

    other = swap(own, "row", 2)
    one = swap(own, "row", 4)
    three = swap(own, "row", 12)
    rows = hours(place, parts, [own])
    rows_one = swap(rows, "col", 1)
    rows_three = swap(rows, "col", 3)

    up, down = relay(other, one, three, rows)
    near = stack(own, other, one, three)
    up = swap(up, "row", 4)
    down = swap(down, "row", 12)
    other_two = swap(other, "row", 8)
    far_low = swap(rows_one[:1], "col", 3)
    far_high = swap(rows_three[1:], "col", 1)
    left = left_near(place, rows, rows_one, rows_three)
    up, down, other_two, left = lax.optimization_barrier((up, down, other_two, left))
    far = stack(up, down, other_two)
    near_core = swap(near, "row", 1)
    far_core = swap(far, "row", 1)

    bin_place = jnp.stack([col, k]).astype(jnp.int32)
    left = left_far(place, far_low, far_high, left)
    return product(bin_place, left, near, far, near_core, far_core)


def solution(mesh):
    return jax.shard_map(
        per_device,
        mesh=mesh,
        in_specs=(P(None, None, "hour", ("row", "col")), P("hour"), P()),
        out_specs=P("hour", None, "row", "col"),
        check_vma=False,
    )
```

```python
import functools

import jax
import jax.numpy as jnp
from jax import lax
from jax.experimental import pallas as pl
from jax.experimental.pallas import tpu as pltpu
from jax.sharding import PartitionSpec as P

BF = jnp.bfloat16
VMEM = pl.BlockSpec(memory_space=pltpu.VMEM)
SMEM = pl.BlockSpec(memory_space=pltpu.SMEM)
ANY = pl.BlockSpec(memory_space=pl.ANY)


def y_z_core():
    row = lax.axis_index("row")
    return row >> 2, (row >> 1) & 1, row & 1


def struct(*shape):
    return jax.ShapeDtypeStruct(shape, BF)


def call(kernel, name, out_shape, in_specs, *operands, aliases={}, cost=None):
    return pl.pallas_call(
        kernel,
        out_shape=out_shape,
        input_output_aliases=aliases,
        in_specs=in_specs,
        out_specs=[VMEM] * len(out_shape) if isinstance(out_shape, list) else VMEM,
        compiler_params=pltpu.CompilerParams(vmem_limit_bytes=6 * 1024 * 1024),
        cost_estimate=cost,
        name=name,
    )(*operands)


def whiten_kernel(spectra, quality, white, spread):
    values = spectra[...].astype(jnp.float32)
    power = jnp.sum(jnp.sum(values * values, axis=0), axis=0) * (1.0 / 16.0)
    scale = lax.rsqrt(power + 1e-06)
    keep = jnp.broadcast_to(quality[...].astype(jnp.float32), (128, 64)).T
    result = (values * keep[None, None] * scale[None, None]).astype(BF)
    white[...] = result
    for h in range(4):
        for k in range(2):
            for z in range(2):
                for y in range(4):
                    spread[h, y, z, k] = result[2 * h + k, z, 16 * y : 16 * y + 16]


def whiten(spectra, quality):
    shapes = [struct(8, 2, 64, 128), struct(4, 4, 2, 2, 16, 128)]
    return call(whiten_kernel, "whiten", shapes, [VMEM] * 2, spectra, quality.reshape(1, 64))


def select_kernel(place, pieces, *outs):
    for d in range(4):
        group = place[0] ^ d
        for s in range(4):
            index = place[1 + group * 4 + s]
            for h in range(4):
                outs[d][16 * h : 16 * h + 16, 128 * s : 128 * s + 128] = pieces[h, index]


def select(place, pieces):
    return call(select_kernel, "select", [struct(64, 512)] * 4, [SMEM, VMEM], place, pieces)


def merge_kernel(*refs):
    out, col = refs[-1], lax.axis_index("col")
    for d in range(4):
        quarter = col ^ d
        for s in range(4):
            at = pl.multiple_of(s * 512 + quarter * 128, 128)
            out[:, pl.ds(at, 128)] = refs[d][:, 128 * s : 128 * s + 128]


def merge(parts, after):
    specs = [VMEM] * (4 + len(after))
    return call(merge_kernel, "merge", struct(64, 2048), specs, *parts, *after)


def relay_kernel(other, one, three, after, up, down):
    up[0:64] = other[...]
    up[64:96] = three[0:32]
    down[0:64] = other[...]
    down[64:96] = one[32:64]


def relay(*parts):
    return call(relay_kernel, "relay", [struct(96, 2048)] * 2, [VMEM] * 4, *parts)


def stack_kernel(*refs):
    out, at = refs[-1], 0
    for ref in refs[:-1]:
        rows = ref.shape[0]
        out[at : at + rows] = ref[...]
        at += rows


def stack(*parts):
    return call(stack_kernel, "stack", struct(256, 2048), [VMEM] * len(parts), *parts)


def hours_kernel(*refs):
    out = refs[-1]
    own_hour, y = lax.axis_index("hour"), y_z_core()[0]
    for d in range(4):
        hour = own_hour ^ d
        for i, dy in enumerate((0, 1, 3, 2)):
            at = pl.multiple_of(64 * i + hour * 16, 16)
            taken = pl.ds(pl.multiple_of((y ^ dy) * 16, 16), 16)
            out[:, :, pl.ds(at, 16)] = refs[d][:, :, taken]


def hours(parts, after):
    specs = [VMEM] * (4 + len(after))
    return call(hours_kernel, "hours", struct(2, 2, 256, 128), specs, *parts, *after)


WINDOWS = (
    (0, 0, 64), (1, 0, 64), (0, 64, 128), (0, 128, 192), (1, 64, 128),
    (0, 192, 224), (1, 128, 192), (0, 224, 256), (1, 192, 256),
)


def put_left(out, f, d, ref, ref_f):
    z = y_z_core()[1]
    rows = ref[ref_f, z] * 0.0625, ref[ref_f, 1 - z] * 0.0625
    sign = jnp.where(z == 0, 1.0, -1.0)
    signed = (rows[1] * sign).astype(BF), (rows[0] * -sign).astype(BF)
    for part, of in enumerate((rows, signed)):
        ordered = jnp.concatenate([of[side][a:b] for side, a, b in WINDOWS], axis=0)
        out[f, part, 128 * d : 128 * d + 128] = ordered.T


def left_near_kernel(*refs):
    for d, ref in enumerate(refs[:3]):
        for f in range(2):
            put_left(refs[3], f, d, ref, f)


def left_near(*parts):
    return call(left_near_kernel, "left_near", struct(2, 2, 512, 512), [VMEM] * 3, *parts)


def halves_kernel(one, three, low, high):
    low[0] = one[0]
    high[0] = three[1]


def halves(*parts):
    cost = pl.CostEstimate(flops=4_000_000_000, bytes_accessed=1 << 20, transcendentals=0)
    return call(halves_kernel, "halves", [struct(1, 2, 256, 128)] * 2, [VMEM] * 2, *parts, cost=cost)


def left_far_kernel(low, high, left, out):
    for f, ref in enumerate((low, high)):
        put_left(out, f, 3, ref, 0)


def left_far(*parts):
    cost = pl.CostEstimate(flops=50_000_000_000, bytes_accessed=1 << 20, transcendentals=0)
    return call(left_far_kernel, "left_far", struct(2, 2, 512, 512), [VMEM] * 3, *parts, aliases={2: 0}, cost=cost)


WIDE, STRIPS = 512, 4


def product_kernel(left, *refs):
    col, core = lax.axis_index("col"), y_z_core()[2]
    out, held, sem = refs[4:]
    copies = []
    for n in range(2):
        near, far = refs[2 * n : 2 * n + 2]
        f = core ^ n
        both = left[f].reshape(1024, 512)
        for j in range(STRIPS):
            columns = slice(WIDE * j, WIDE * j + WIDE)
            right = jnp.concatenate([near[:, columns], far[:, columns]], axis=0)
            result = jnp.dot(both, right, preferred_element_type=jnp.float32)
            held[n, j] = result.astype(BF).reshape(2, 512, WIDE)
            for i, d in enumerate((0, 1, 3, 2)):
                rows = pl.ds(pl.multiple_of((col ^ d) * 128, 128), 128)
                copy = pltpu.make_async_copy(
                    held.at[n, j, :, pl.ds(128 * i, 128)], out.at[f, :, rows, columns], sem.at[n, j, i]
                )
                copy.start()
                copies.append(copy)
    for copy in copies:
        copy.wait()


def product(*operands):
    return pl.pallas_call(
        product_kernel,
        out_shape=struct(2, 2, 512, 2048),
        in_specs=[VMEM] * 5,
        out_specs=ANY,
        scratch_shapes=[
            pltpu.VMEM((2, STRIPS, 2, 512, WIDE), BF),
            pltpu.SemaphoreType.DMA((2, STRIPS, 4)),
        ],
        compiler_params=pltpu.CompilerParams(vmem_limit_bytes=16 * 1024 * 1024),
        name="product",
    )(*operands)


def swap(value, axis, bits):
    return lax.ppermute(value, axis, [(i, i ^ bits) for i in range(lax.axis_size(axis))])


def per_device(spectra, quality, column_blocks):
    col, hour = lax.axis_index("col"), lax.axis_index("hour")
    place = jnp.concatenate([col.astype(jnp.int32).reshape(1), column_blocks])
    white, spread = whiten(spectra, quality)
    parts = [lax.dynamic_slice_in_dim(white, 2 * (hour ^ d), 2, 0) for d in range(4)]
    parts = [parts[0]] + [swap(parts[d], "hour", d) for d in range(1, 4)]

    pieces = lax.all_to_all(spread.reshape(64, 16, 128), ("hour", "row"), 0, 0, tiled=True)
    sent = select(place, pieces.reshape(4, 16, 16, 128))
    sent = [sent[0]] + [swap(sent[d], "col", d) for d in range(1, 4)]
    own = merge(sent, parts[1:])

    other = swap(own, "row", 2)
    one = swap(own, "row", 4)
    three = swap(own, "row", 12)
    rows = hours(parts, [own])
    rows_one = swap(rows, "col", 1)
    rows_three = swap(rows, "col", 3)

    up, down = relay(other, one, three, rows)
    near = stack(own, other, one, three)
    up = swap(up, "row", 4)
    down = swap(down, "row", 12)
    other_two = swap(other, "row", 8)
    far_low, far_high = halves(rows_one, rows_three)
    far_low = swap(far_low, "col", 3)
    far_high = swap(far_high, "col", 1)
    left = left_near(rows, rows_one, rows_three)
    up, down, other_two, left = lax.optimization_barrier((up, down, other_two, left))
    far = stack(up, down, other_two)
    near_core = swap(near, "row", 1)
    far_core = swap(far, "row", 1)

    left = left_far(far_low, far_high, left)
    return product(left, near, far, near_core, far_core)


def solution(mesh):
    return jax.shard_map(
        per_device,
        mesh=mesh,
        in_specs=(P(None, None, "hour", ("row", "col")), P("hour"), P()),
        out_specs=P("hour", None, "row", "col"),
        check_vma=False,
    )
```

```python
import functools

import jax
import jax.numpy as jnp
from jax import lax
from jax.experimental import pallas as pl
from jax.experimental.pallas import tpu as pltpu
from jax.sharding import PartitionSpec as P

BF = jnp.bfloat16
VMEM = pl.BlockSpec(memory_space=pltpu.VMEM)
SMEM = pl.BlockSpec(memory_space=pltpu.SMEM)
ANY = pl.BlockSpec(memory_space=pl.ANY)


def y_z_core():
    row = lax.axis_index("row")
    return row >> 2, (row >> 1) & 1, row & 1


def struct(*shape):
    return jax.ShapeDtypeStruct(shape, BF)


def call(kernel, name, out_shape, in_specs, *operands, aliases={}, cost=None):
    return pl.pallas_call(
        kernel,
        out_shape=out_shape,
        input_output_aliases=aliases,
        in_specs=in_specs,
        out_specs=[VMEM] * len(out_shape) if isinstance(out_shape, list) else VMEM,
        compiler_params=pltpu.CompilerParams(vmem_limit_bytes=6 * 1024 * 1024),
        cost_estimate=cost,
        name=name,
    )(*operands)


def whiten_kernel(spectra, quality, white, spread):
    values = spectra[...].astype(jnp.float32)
    power = jnp.sum(jnp.sum(values * values, axis=0), axis=0) * (1.0 / 16.0)
    scale = lax.rsqrt(power + 1e-06)
    keep = jnp.broadcast_to(quality[...].astype(jnp.float32), (128, 64)).T
    result = (values * keep[None, None] * scale[None, None]).astype(BF)
    white[...] = result
    for h in range(4):
        for k in range(2):
            for z in range(2):
                for y in range(4):
                    spread[y, z, k, h] = result[2 * h + k, z, 16 * y : 16 * y + 16]


def whiten(spectra, quality):
    shapes = [struct(8, 2, 64, 128), struct(4, 2, 2, 4, 16, 128)]
    return call(whiten_kernel, "whiten", shapes, [VMEM] * 2, spectra, quality.reshape(1, 64))


def select_kernel(place, pieces, *outs):
    for d in range(4):
        group = place[0] ^ d
        for s in range(4):
            index = place[1 + group * 4 + s]
            for h in range(4):
                outs[d][16 * h : 16 * h + 16, 128 * s : 128 * s + 128] = pieces[index, h]


def select(place, pieces):
    return call(select_kernel, "select", [struct(64, 512)] * 4, [SMEM, VMEM], place, pieces)


def merge_kernel(*refs):
    out, col = refs[-1], lax.axis_index("col")
    for d in range(4):
        quarter = col ^ d
        for s in range(4):
            at = pl.multiple_of(s * 512 + quarter * 128, 128)
            out[:, pl.ds(at, 128)] = refs[d][:, 128 * s : 128 * s + 128]


def merge(parts, after):
    specs = [VMEM] * (4 + len(after))
    return call(merge_kernel, "merge", struct(64, 2048), specs, *parts, *after)


def relay_kernel(three, one, other, after, up, down):
    up[0:64] = other[...]
    up[64:96] = three[0:32]
    down[0:64] = other[...]
    down[64:96] = one[32:64]


def relay(*parts):
    return call(relay_kernel, "relay", [struct(96, 2048)] * 2, [VMEM] * 4, *parts)


def stack_kernel(*refs):
    out, at = refs[-1], 0
    for ref in refs[:-1]:
        rows = ref.shape[0]
        out[at : at + rows] = ref[...]
        at += rows


def stack(*parts):
    shape = struct(sum(part.shape[0] for part in parts), 2048)
    return call(stack_kernel, "stack", shape, [VMEM] * len(parts), *parts)


def hours_kernel(*refs):
    out = refs[-1]
    own_hour, y = lax.axis_index("hour"), y_z_core()[0]
    for d in range(4):
        hour = own_hour ^ d
        for i, dy in enumerate((0, 1, 3, 2)):
            at = pl.multiple_of(64 * i + hour * 16, 16)
            taken = pl.ds(pl.multiple_of((y ^ dy) * 16, 16), 16)
            out[:, :, pl.ds(at, 16)] = refs[d][:, :, taken]


def hours(parts, after):
    specs = [VMEM] * (4 + len(after))
    return call(hours_kernel, "hours", struct(2, 2, 256, 128), specs, *parts, *after)


WINDOWS = (
    (0, 0, 64), (1, 0, 64), (0, 64, 128), (0, 128, 192), (1, 192, 256),
    (1, 64, 128), (0, 192, 224), (1, 128, 192), (0, 224, 256),
)


def put_left(out, f, d, ref, ref_f):
    z = y_z_core()[1]
    rows = ref[ref_f, z] * 0.0625, ref[ref_f, 1 - z] * 0.0625
    sign = jnp.where(z == 0, 1.0, -1.0)
    signed = (rows[1] * sign).astype(BF), (rows[0] * -sign).astype(BF)
    for part, of in enumerate((rows, signed)):
        ordered = jnp.concatenate([of[side][a:b] for side, a, b in WINDOWS], axis=0)
        out[f, part, 128 * d : 128 * d + 128] = ordered.T


def left_near_kernel(*refs):
    for d, ref in enumerate(refs[:3]):
        for f in range(2):
            put_left(refs[3], f, d, ref, f)


def left_near(*parts):
    return call(left_near_kernel, "left_near", struct(2, 2, 512, 512), [VMEM] * 3, *parts)


def halves_kernel(one, three, low, high):
    low[0] = one[0]
    high[0] = three[1]


def halves(*parts):
    cost = pl.CostEstimate(flops=4_000_000_000, bytes_accessed=1 << 20, transcendentals=0)
    return call(halves_kernel, "halves", [struct(1, 2, 256, 128)] * 2, [VMEM] * 2, *parts, cost=cost)


def left_far_kernel(low, high, left, out):
    for f, ref in enumerate((low, high)):
        put_left(out, f, 3, ref, 0)


def left_far(*parts):
    cost = pl.CostEstimate(flops=50_000_000_000, bytes_accessed=1 << 20, transcendentals=0)
    return call(left_far_kernel, "left_far", struct(2, 2, 512, 512), [VMEM] * 3, *parts, aliases={2: 0}, cost=cost)


WIDE, STRIPS = 512, 4


def product_kernel(other, left, near, far, *refs):
    out, held, sem = refs[-3:]
    col, f = lax.axis_index("col"), y_z_core()[2] ^ other
    copies = []
    both = left[f].reshape(1024, 512)
    for j in range(STRIPS):
        columns = slice(WIDE * j, WIDE * j + WIDE)
        right = jnp.concatenate([near[:, columns], far[:, columns]], axis=0)
        result = jnp.dot(both, right, preferred_element_type=jnp.float32)
        held[j] = result.astype(BF).reshape(2, 512, WIDE)
        for i, d in enumerate((0, 1, 3, 2)):
            rows = pl.ds(pl.multiple_of((col ^ d) * 128, 128), 128)
            copy = pltpu.make_async_copy(
                held.at[j, :, pl.ds(128 * i, 128)], out.at[f, :, rows, columns], sem.at[j, i]
            )
            copy.start()
            copies.append(copy)
    for copy in copies:
        copy.wait()


def product(other, *operands):
    return pl.pallas_call(
        functools.partial(product_kernel, other),
        out_shape=struct(2, 2, 512, 2048),
        in_specs=[VMEM] * 3 + [ANY] * other,
        out_specs=ANY,
        input_output_aliases={3: 0} if other else {},
        scratch_shapes=[pltpu.VMEM((STRIPS, 2, 512, WIDE), BF), pltpu.SemaphoreType.DMA((STRIPS, 4))],
        compiler_params=pltpu.CompilerParams(vmem_limit_bytes=10 * 1024 * 1024),
        name="product",
    )(*operands)


def swap(value, axis, bits):
    return lax.ppermute(value, axis, [(i, i ^ bits) for i in range(lax.axis_size(axis))])


def per_device(spectra, quality, column_blocks):
    col, hour = lax.axis_index("col"), lax.axis_index("hour")
    place = jnp.concatenate([col.astype(jnp.int32).reshape(1), column_blocks])
    white, spread = whiten(spectra, quality)
    parts = [lax.dynamic_slice_in_dim(white, 2 * (hour ^ d), 2, 0) for d in range(4)]
    parts = [parts[0]] + [swap(parts[d], "hour", d) for d in range(1, 4)]

    pieces = lax.all_to_all(spread.reshape(64, 16, 128), ("row", "hour"), 0, 0, tiled=True)
    sent = select(place, pieces.reshape(16, 4, 16, 128))
    sent = [sent[0]] + [swap(sent[d], "col", d) for d in range(1, 4)]
    own = merge(sent, parts[1:])

    three = swap(own, "row", 12)
    one = swap(own, "row", 4)
    other = swap(own, "row", 2)
    rows = hours(parts, [own])
    rows_one = swap(rows, "col", 1)
    rows_three = swap(rows, "col", 3)

    up, down = relay(three, one, other, rows)
    up = swap(up, "row", 4)
    down = swap(down, "row", 12)
    other_two = swap(other, "row", 8)
    far_low, far_high = halves(rows_one, rows_three)
    far_low = swap(far_low, "col", 3)
    far_high = swap(far_high, "col", 1)
    left = left_near(rows, rows_one, rows_three)
    up, down, left = lax.optimization_barrier((up, down, left))
    near = stack(own, other, one, three, other_two)
    far = stack(up, down)
    near_core = swap(near, "row", 1)
    far_core = swap(far, "row", 1)

    left = left_far(far_low, far_high, left)
    out = product(0, left, near, far)
    return product(1, left, near_core, far_core, out)


def solution(mesh):
    return jax.shard_map(
        per_device,
        mesh=mesh,
        in_specs=(P(None, None, "hour", ("row", "col")), P("hour"), P()),
        out_specs=P("hour", None, "row", "col"),
        check_vma=False,
    )
```

```python
import functools

import jax
import jax.numpy as jnp
from jax import lax
from jax.experimental import pallas as pl
from jax.experimental.pallas import tpu as pltpu
from jax.sharding import PartitionSpec as P

BF = jnp.bfloat16
VMEM = pl.BlockSpec(memory_space=pltpu.VMEM)
SMEM = pl.BlockSpec(memory_space=pltpu.SMEM)
ANY = pl.BlockSpec(memory_space=pl.ANY)


def y_z_core():
    row = lax.axis_index("row")
    return row >> 2, (row >> 1) & 1, row & 1


def struct(*shape):
    return jax.ShapeDtypeStruct(shape, BF)


def call(kernel, name, out_shape, in_specs, *operands, aliases={}, cost=None):
    return pl.pallas_call(
        kernel,
        out_shape=out_shape,
        input_output_aliases=aliases,
        in_specs=in_specs,
        out_specs=[VMEM] * len(out_shape) if isinstance(out_shape, list) else VMEM,
        compiler_params=pltpu.CompilerParams(vmem_limit_bytes=6 * 1024 * 1024),
        cost_estimate=cost,
        name=name,
    )(*operands)


def whiten_kernel(spectra, quality, white, spread):
    values = spectra[...].astype(jnp.float32)
    power = jnp.sum(jnp.sum(values * values, axis=0), axis=0) * (1.0 / 16.0)
    scale = lax.rsqrt(power + 1e-06)
    keep = jnp.broadcast_to(quality[...].astype(jnp.float32), (128, 64)).T
    result = (values * keep[None, None] * scale[None, None]).astype(BF)
    white[...] = result
    for h in range(4):
        for k in range(2):
            for z in range(2):
                for y in range(4):
                    spread[y, z, k, h] = result[2 * h + k, z, 16 * y : 16 * y + 16]


def whiten(spectra, quality):
    shapes = [struct(8, 2, 64, 128), struct(4, 2, 2, 4, 16, 128)]
    return call(whiten_kernel, "whiten", shapes, [VMEM] * 2, spectra, quality.reshape(1, 64))


def select_kernel(place, pieces, *outs):
    for d in range(4):
        group = place[0] ^ d
        for s in range(4):
            index = place[1 + group * 4 + s]
            for h in range(4):
                outs[d][16 * h : 16 * h + 16, 128 * s : 128 * s + 128] = pieces[index, h]


def select(place, pieces):
    return call(select_kernel, "select", [struct(64, 512)] * 4, [SMEM, VMEM], place, pieces)


def merge_kernel(*refs):
    out, col = refs[-1], lax.axis_index("col")
    for i, d in enumerate((0, 2, 3, 1)):
        quarter = col ^ d
        for s in range(4):
            at = pl.multiple_of(s * 512 + quarter * 128, 128)
            out[:, pl.ds(at, 128)] = refs[i][:, 128 * s : 128 * s + 128]


def merge(parts, after):
    specs = [VMEM] * (4 + len(after))
    return call(merge_kernel, "merge", struct(64, 2048), specs, *parts, *after)


def relay_kernel(three, one, other, after, up, down):
    up[0:64] = other[...]
    up[64:96] = three[0:32]
    down[0:64] = other[...]
    down[64:96] = one[32:64]


def relay(*parts):
    return call(relay_kernel, "relay", [struct(96, 2048)] * 2, [VMEM] * 4, *parts)


def stack_kernel(*refs):
    out, at = refs[-1], 0
    for ref in refs[:-1]:
        rows = ref.shape[0]
        out[at : at + rows] = ref[...]
        at += rows


def stack(*parts):
    shape = struct(sum(part.shape[0] for part in parts), 2048)
    return call(stack_kernel, "stack", shape, [VMEM] * len(parts), *parts)


def hours_kernel(*refs):
    out = refs[-1]
    own_hour, y = lax.axis_index("hour"), y_z_core()[0]
    for d in range(4):
        hour = own_hour ^ d
        for i, dy in enumerate((0, 1, 3, 2)):
            at = pl.multiple_of(64 * i + hour * 16, 16)
            taken = pl.ds(pl.multiple_of((y ^ dy) * 16, 16), 16)
            out[:, :, pl.ds(at, 16)] = refs[d][:, :, taken]


def hours(parts, after):
    specs = [VMEM] * (4 + len(after))
    return call(hours_kernel, "hours", struct(2, 2, 256, 128), specs, *parts, *after)


WINDOWS = (
    (0, 0, 64), (1, 0, 64), (0, 64, 128), (0, 128, 192), (1, 192, 256),
    (1, 64, 128), (0, 192, 224), (1, 128, 192), (0, 224, 256),
)


def put_left(out, f, d, ref, ref_f):
    z = y_z_core()[1]
    rows = ref[ref_f, z] * 0.0625, ref[ref_f, 1 - z] * 0.0625
    sign = jnp.where(z == 0, 1.0, -1.0)
    signed = (rows[1] * sign).astype(BF), (rows[0] * -sign).astype(BF)
    for part, of in enumerate((rows, signed)):
        ordered = jnp.concatenate([of[side][a:b] for side, a, b in WINDOWS], axis=0)
        out[f, part, 128 * d : 128 * d + 128] = ordered.T


def left_near_kernel(*refs):
    for d, ref in enumerate(refs[:3]):
        for f in range(2):
            put_left(refs[3], f, d, ref, f)


def left_near(*parts):
    return call(left_near_kernel, "left_near", struct(2, 2, 512, 512), [VMEM] * 3, *parts)


def halves_kernel(one, three, low, high):
    low[0] = one[0]
    high[0] = three[1]


def halves(*parts):
    cost = pl.CostEstimate(flops=4_000_000_000, bytes_accessed=1 << 20, transcendentals=0)
    return call(halves_kernel, "halves", [struct(1, 2, 256, 128)] * 2, [VMEM] * 2, *parts, cost=cost)


def left_far_kernel(low, high, left, out):
    for f, ref in enumerate((low, high)):
        put_left(out, f, 3, ref, 0)


def left_far(*parts):
    cost = pl.CostEstimate(flops=50_000_000_000, bytes_accessed=1 << 20, transcendentals=0)
    return call(left_far_kernel, "left_far", struct(2, 2, 512, 512), [VMEM] * 3, *parts, aliases={2: 0}, cost=cost)


WIDE, STRIPS = 512, 4


def product_kernel(other, left, near, far, *refs):
    out, held, sem = refs[-3:]
    col, f = lax.axis_index("col"), y_z_core()[2] ^ other
    copies = []
    both = left[f].reshape(1024, 512)
    for j in range(STRIPS):
        columns = slice(WIDE * j, WIDE * j + WIDE)
        right = jnp.concatenate([near[:, columns], far[:, columns]], axis=0)
        result = jnp.dot(both, right, preferred_element_type=jnp.float32)
        held[j] = result.astype(BF).reshape(2, 512, WIDE)
        for i, d in enumerate((0, 1, 3, 2)):
            rows = pl.ds(pl.multiple_of((col ^ d) * 128, 128), 128)
            copy = pltpu.make_async_copy(
                held.at[j, :, pl.ds(128 * i, 128)], out.at[f, :, rows, columns], sem.at[j, i]
            )
            copy.start()
            copies.append(copy)
    for copy in copies:
        copy.wait()


def product(other, *operands):
    return pl.pallas_call(
        functools.partial(product_kernel, other),
        out_shape=struct(2, 2, 512, 2048),
        in_specs=[VMEM] * 3 + [ANY] * other,
        out_specs=ANY,
        input_output_aliases={3: 0} if other else {},
        scratch_shapes=[pltpu.VMEM((STRIPS, 2, 512, WIDE), BF), pltpu.SemaphoreType.DMA((STRIPS, 4))],
        compiler_params=pltpu.CompilerParams(vmem_limit_bytes=10 * 1024 * 1024),
        name="product",
    )(*operands)


def swap(value, axis, bits):
    return lax.ppermute(value, axis, [(i, i ^ bits) for i in range(lax.axis_size(axis))])


def per_device(spectra, quality, column_blocks):
    col, hour = lax.axis_index("col"), lax.axis_index("hour")
    place = jnp.concatenate([col.astype(jnp.int32).reshape(1), column_blocks])
    white, spread = whiten(spectra, quality)
    parts = [lax.dynamic_slice_in_dim(white, 2 * (hour ^ d), 2, 0) for d in range(4)]
    parts = [parts[0]] + [swap(parts[d], "hour", d) for d in range(1, 4)]

    pieces = lax.all_to_all(spread.reshape(64, 16, 128), ("row", "hour"), 0, 0, tiled=True)
    sent = select(place, pieces.reshape(16, 4, 16, 128))
    moved = {d: swap(sent[d], "col", d) for d in (1, 3, 2)}
    sent = [sent[0]] + [moved[d] for d in range(1, 4)]
    own = merge([sent[0], sent[2], sent[3], sent[1]], parts[1:])

    three = swap(own, "row", 12)
    one = swap(own, "row", 4)
    other = swap(own, "row", 2)
    rows = hours(parts, [own])
    rows_one = swap(rows, "col", 1)
    rows_three = swap(rows, "col", 3)

    up, down = relay(three, one, other, rows)
    up = swap(up, "row", 4)
    down = swap(down, "row", 12)
    other_two = swap(other, "row", 8)
    far_low, far_high = halves(rows_one, rows_three)
    far_low = swap(far_low, "col", 3)
    far_high = swap(far_high, "col", 1)
    left = left_near(rows, rows_one, rows_three)
    up, down, left = lax.optimization_barrier((up, down, left))
    near = stack(own, other, one, three, other_two)
    far = stack(up, down)
    near_core = swap(near, "row", 1)
    far_core = swap(far, "row", 1)

    left = left_far(far_low, far_high, left)
    out = product(0, left, near, far)
    return product(1, left, near_core, far_core, out)


def solution(mesh):
    return jax.shard_map(
        per_device,
        mesh=mesh,
        in_specs=(P(None, None, "hour", ("row", "col")), P("hour"), P()),
        out_specs=P("hour", None, "row", "col"),
        check_vma=False,
    )
```

```python
import functools

import jax
import jax.numpy as jnp
from jax import lax
from jax.experimental import pallas as pl
from jax.experimental.pallas import tpu as pltpu
from jax.sharding import PartitionSpec as P

BF = jnp.bfloat16
VMEM = pl.BlockSpec(memory_space=pltpu.VMEM)
SMEM = pl.BlockSpec(memory_space=pltpu.SMEM)
ANY = pl.BlockSpec(memory_space=pl.ANY)


def y_z_core():
    row = lax.axis_index("row")
    return row >> 2, (row >> 1) & 1, row & 1


def struct(*shape):
    return jax.ShapeDtypeStruct(shape, BF)


def call(kernel, name, out_shape, in_specs, *operands, aliases={}, cost=None):
    return pl.pallas_call(
        kernel,
        out_shape=out_shape,
        input_output_aliases=aliases,
        in_specs=in_specs,
        out_specs=[VMEM] * len(out_shape) if isinstance(out_shape, list) else VMEM,
        compiler_params=pltpu.CompilerParams(vmem_limit_bytes=6 * 1024 * 1024),
        cost_estimate=cost,
        name=name,
    )(*operands)


def whiten_kernel(spectra, quality, white, spread):
    values = spectra[...].astype(jnp.float32)
    power = jnp.sum(jnp.sum(values * values, axis=0), axis=0) * (1.0 / 16.0)
    scale = lax.rsqrt(power + 1e-06)
    keep = jnp.broadcast_to(quality[...].astype(jnp.float32), (128, 64)).T
    result = (values * keep[None, None] * scale[None, None]).astype(BF)
    white[...] = result
    for h in range(4):
        for k in range(2):
            for z in range(2):
                for y in range(4):
                    spread[y, z, k, h] = result[2 * h + k, z, 16 * y : 16 * y + 16]


def whiten(spectra, quality):
    shapes = [struct(8, 2, 64, 128), struct(4, 2, 2, 4, 16, 128)]
    return call(whiten_kernel, "whiten", shapes, [VMEM] * 2, spectra, quality.reshape(1, 64))


def select_kernel(place, pieces, *outs):
    for d in range(4):
        group = place[0] ^ d
        for s in range(4):
            index = place[1 + group * 4 + s]
            for h in range(4):
                outs[d][16 * h : 16 * h + 16, 128 * s : 128 * s + 128] = pieces[index, h]


def select(place, pieces):
    return call(select_kernel, "select", [struct(64, 512)] * 4, [SMEM, VMEM], place, pieces)


def merge_kernel(*refs):
    out, col = refs[-1], lax.axis_index("col")
    for i, d in enumerate((0, 2, 3, 1)):
        quarter = col ^ d
        for s in range(4):
            at = pl.multiple_of(s * 512 + quarter * 128, 128)
            out[:, pl.ds(at, 128)] = refs[i][:, 128 * s : 128 * s + 128]


def merge(parts, after):
    specs = [VMEM] * (4 + len(after))
    return call(merge_kernel, "merge", struct(64, 2048), specs, *parts, *after)


def relay_kernel(three, one, other, after, up, down):
    up[0:64] = other[...]
    up[64:96] = three[0:32]
    down[0:64] = other[...]
    down[64:96] = one[32:64]


def relay(*parts):
    return call(relay_kernel, "relay", [struct(96, 2048)] * 2, [VMEM] * 4, *parts)


def stack_kernel(*refs):
    out, at = refs[-1], 0
    for ref in refs[:-1]:
        rows = ref.shape[0]
        out[at : at + rows] = ref[...]
        at += rows


def stack(*parts):
    shape = struct(sum(part.shape[0] for part in parts), 2048)
    return call(stack_kernel, "stack", shape, [VMEM] * len(parts), *parts)


def hours_kernel(*refs):
    out = refs[-1]
    own_hour, y = lax.axis_index("hour"), y_z_core()[0]
    for d in range(4):
        hour = own_hour ^ d
        for i, dy in enumerate((0, 1, 3, 2)):
            at = pl.multiple_of(64 * i + hour * 16, 16)
            taken = pl.ds(pl.multiple_of((y ^ dy) * 16, 16), 16)
            out[:, :, pl.ds(at, 16)] = refs[d][:, :, taken]


def hours(parts, after):
    specs = [VMEM] * (4 + len(after))
    return call(hours_kernel, "hours", struct(2, 2, 256, 128), specs, *parts, *after)


WINDOWS = (
    (0, 0, 64), (1, 0, 64), (0, 64, 128), (0, 128, 192), (1, 192, 256),
    (1, 64, 128), (0, 192, 224), (1, 128, 192), (0, 224, 256),
)


def put_left(out, f, d, ref, ref_f):
    z = y_z_core()[1]
    rows = ref[ref_f, z] * 0.0625, ref[ref_f, 1 - z] * 0.0625
    sign = jnp.where(z == 0, 1.0, -1.0)
    signed = (rows[1] * sign).astype(BF), (rows[0] * -sign).astype(BF)
    for part, of in enumerate((rows, signed)):
        ordered = jnp.concatenate([of[side][a:b] for side, a, b in WINDOWS], axis=0)
        out[f, part, 128 * d : 128 * d + 128] = ordered.T


def left_near_kernel(*refs):
    for d, ref in enumerate(refs[:3]):
        for f in range(2):
            put_left(refs[3], f, d, ref, f)


def left_near(*parts):
    return call(left_near_kernel, "left_near", struct(2, 2, 512, 512), [VMEM] * 3, *parts)


def halves_kernel(one, three, low, high):
    low[0] = one[0]
    high[0] = three[1]


def halves(*parts):
    cost = pl.CostEstimate(flops=4_000_000_000, bytes_accessed=1 << 20, transcendentals=0)
    return call(halves_kernel, "halves", [struct(1, 2, 256, 128)] * 2, [VMEM] * 2, *parts, cost=cost)


def left_far_kernel(low, high, left, out):
    for f, ref in enumerate((low, high)):
        put_left(out, f, 3, ref, 0)


def left_far(*parts):
    cost = pl.CostEstimate(flops=50_000_000_000, bytes_accessed=1 << 20, transcendentals=0)
    return call(left_far_kernel, "left_far", struct(2, 2, 512, 512), [VMEM] * 3, *parts, aliases={2: 0}, cost=cost)


WIDE, STRIPS = 512, 4


def product_kernel(other, left, near, far, *refs):
    out, held, sem = refs[-3:]
    col, f = lax.axis_index("col"), y_z_core()[2] ^ other
    copies = []
    both = left[f].reshape(1024, 512)
    for j in range(STRIPS):
        columns = slice(WIDE * j, WIDE * j + WIDE)
        right = jnp.concatenate([near[:, columns], far[:, columns]], axis=0)
        last = j == STRIPS - 1
        for n in range(2 if last else 1):
            parts = slice(n, n + 1) if last else slice(0, 2)
            count = parts.stop - parts.start
            some = left[f, parts].reshape(512 * count, 512) if last else both
            result = jnp.dot(some, right, preferred_element_type=jnp.float32)
            held[j, parts] = result.astype(BF).reshape(count, 512, WIDE)
            for i, d in enumerate((0, 1, 3, 2)):
                rows = pl.ds(pl.multiple_of((col ^ d) * 128, 128), 128)
                copy = pltpu.make_async_copy(
                    held.at[j, parts, pl.ds(128 * i, 128)], out.at[f, parts, rows, columns], sem.at[j + n, i]
                )
                copy.start()
                copies.append(copy)
    for copy in copies:
        copy.wait()


def product(other, *operands):
    return pl.pallas_call(
        functools.partial(product_kernel, other),
        out_shape=struct(2, 2, 512, 2048),
        in_specs=[VMEM] * 3 + [ANY] * other,
        out_specs=ANY,
        input_output_aliases={3: 0} if other else {},
        scratch_shapes=[pltpu.VMEM((STRIPS, 2, 512, WIDE), BF), pltpu.SemaphoreType.DMA((STRIPS + 1, 4))],
        compiler_params=pltpu.CompilerParams(vmem_limit_bytes=10 * 1024 * 1024),
        name="product",
    )(*operands)


def swap(value, axis, bits):
    return lax.ppermute(value, axis, [(i, i ^ bits) for i in range(lax.axis_size(axis))])


def per_device(spectra, quality, column_blocks):
    col, hour = lax.axis_index("col"), lax.axis_index("hour")
    place = jnp.concatenate([col.astype(jnp.int32).reshape(1), column_blocks])
    white, spread = whiten(spectra, quality)
    parts = [lax.dynamic_slice_in_dim(white, 2 * (hour ^ d), 2, 0) for d in range(4)]
    parts = [parts[0]] + [swap(parts[d], "hour", d) for d in range(1, 4)]

    pieces = lax.all_to_all(spread.reshape(64, 16, 128), ("row", "hour"), 0, 0, tiled=True)
    sent = select(place, pieces.reshape(16, 4, 16, 128))
    moved = {d: swap(sent[d], "col", d) for d in (1, 3, 2)}
    sent = [sent[0]] + [moved[d] for d in range(1, 4)]
    own = merge([sent[0], sent[2], sent[3], sent[1]], parts[1:])

    three = swap(own, "row", 12)
    one = swap(own, "row", 4)
    other = swap(own, "row", 2)
    rows = hours(parts, [own])
    rows_one = swap(rows, "col", 1)
    rows_three = swap(rows, "col", 3)

    up, down = relay(three, one, other, rows)
    up = swap(up, "row", 4)
    down = swap(down, "row", 12)
    other_two = swap(other, "row", 8)
    far_low, far_high = halves(rows_one, rows_three)
    far_low = swap(far_low, "col", 3)
    far_high = swap(far_high, "col", 1)
    left = left_near(rows, rows_one, rows_three)
    up, down, left = lax.optimization_barrier((up, down, left))
    near = stack(own, other, one, three, other_two)
    far = stack(up, down)
    near_core = swap(near, "row", 1)
    far_core = swap(far, "row", 1)

    left = left_far(far_low, far_high, left)
    out = product(0, left, near, far)
    return product(1, left, near_core, far_core, out)


def solution(mesh):
    return jax.shard_map(
        per_device,
        mesh=mesh,
        in_specs=(P(None, None, "hour", ("row", "col")), P("hour"), P()),
        out_specs=P("hour", None, "row", "col"),
        check_vma=False,
    )
```
